32 devices in a mesh: row: 8 (over y, x, core), col: 4 (over z).
Axes of the slice: x: 2, y: 2, z: 4, core: 2. Of those that a mesh axis runs over, the one named last changes fastest.
Arguments:
- q_child: float32 [16384, 32768], P('row', 'col'), may hold values from -6 to 6
- sec_weights: float32 [65536, 256], P(('row', 'col')), may hold values from -3000 to 3000
- deflated: int32 [65536], P(('row', 'col')), may hold values 0 or 1
- local_perm: int32 [32, 2048], P(('row', 'col')), may hold values from 0 to 2047, each once within a row
- owner_order: int32 [2, 4], replicated, may hold values from 0 to 3, each once within a row
Outputs:
- merged: float32 [16384, 256], P(('row', 'col'))
The draws below stay inside these ranges and needn't reach their ends.
Inputs may be any that keep to these rules, and one draw needn't show every extreme that they name: `local_perm`: each row is a permutation of 0 to 2047. `owner_order`: each row is a permutation of 0 to 3.
All inputs are finite; a program needn't handle non-finite values. No bound on the sum of `deflated` on one device may be relied on, other than what follows from the above.
Results may differ from the reference program's by a relative error of at most 0.000073.
Values sent between devices are 32-bit elements; how exact they have to be, the bound alone decides.
A program may use at most 192 MiB of HBM per device.

```python
import math
import jax
import jax.numpy as jnp
from jax import lax

ORDER = 65536
HALF_ORDER = 32768
SLAB = 16384
COLS = 256
PIECES = 32
PIECE = 2048
N_ROW = 8
N_COL = 4


def draw_sec_weights(key, part):
    key = jax.random.fold_in(key, 7)
    first_key, second_key, third_key = jax.random.split(key, 3)
    position = jnp.arange(ORDER, dtype=jnp.float32)[:, None] / ORDER
    row_scale = jnp.exp(jax.random.uniform(second_key, (ORDER, 1), minval=0.0, maxval=math.log(10.0)))
    col_scale = jnp.exp(jax.random.uniform(third_key, (1, COLS), minval=0.0, maxval=math.log(10.0)))
    base = jax.random.truncated_normal(first_key, -4.0, 4.0, (ORDER, COLS))
    rising = jnp.exp(position * math.log(3.0))
    return (base * row_scale * col_scale * rising).astype(jnp.float32)


def plant(values, rng, smallest, top_value):
    longest = values.shape.index(max(values.shape))
    spots = []
    for shift in (0, 1):
        where = [jax.random.randint(jax.random.fold_in(rng, axis), (), 0, length) for axis, length in enumerate(values.shape)]
        where[longest] = (where[longest] + shift) % values.shape[longest]
        spots.append(tuple(where))
    return values.at[spots[0]].set(smallest).at[spots[1]].set(top_value)


def raised(values, rng, source, target, blocks, factor):
    owner, partner = [(jnp.arange(values.shape[dim]) // (values.shape[dim] // blocks)).reshape([-1 if axis == dim else 1 for axis in range(values.ndim)]) for dim in (source, target)]
    chosen = jax.random.permutation(rng, blocks)[partner]
    strong = (owner == chosen) | (owner == (partner + blocks // 2) % blocks)
    return jnp.where(strong, factor * values, values)


def block_scale(stream_key, shape, shards, least, top_value):
    loudness, own = 1.0, jax.random.fold_in(stream_key, 6)
    for dim, parts in shards:
        draws = jnp.exp(jax.random.uniform(jax.random.fold_in(own, dim), (parts,), jnp.float32, least / len(shards), top_value / len(shards)))
        loudness = loudness * jnp.repeat(draws, shape[dim] // parts).reshape([-1 if axis == dim else 1 for axis in range(len(shape))])
    return loudness


def bell_draw_with(stream_key, dims, spread, reach, cuts, heavy, kind=jnp.bfloat16):
    array = spread * jax.random.normal(stream_key, dims, jnp.float32)
    if cuts:
        array = array * block_scale(stream_key, dims, cuts, -0.22, 0.18)
    return jnp.clip(raised(array, jax.random.fold_in(stream_key, 3), *heavy), -reach, reach).astype(kind)


def setup_inputs(seed: int = 0) -> dict:
    key_list = jax.random.split(jax.random.key(seed), 6)
    return {
        "q_child": bell_draw_with(key_list[0], (SLAB, HALF_ORDER), 1.0, 6.0, ((0, 8), (1, 4)), (1, 0, 8, 2.0), jnp.float32),
        "sec_weights": draw_sec_weights(jax.random.fold_in(key_list[5], 71), 0),
        "deflated": plant((jax.random.randint(key_list[2], (ORDER,), 0, 4) < 1).astype(jnp.int32), jax.random.fold_in(key_list[2], 1), 0, 1),
        "local_perm": jax.vmap(lambda own: jax.random.permutation(own, PIECE))(jax.random.split(key_list[3], PIECES)).reshape((PIECES, PIECE)).astype(jnp.int32),
        "owner_order": jax.vmap(lambda own: jax.random.permutation(own, N_COL))(jax.random.split(key_list[4], 2)).reshape((2, N_COL)).astype(jnp.int32),
    }


def reference(q_child, sec_weights, deflated, local_perm, owner_order):
    kept_rows = (1 - deflated).astype(jnp.float32)[:, None]
    masked = sec_weights * kept_rows
    col_total = lax.optimization_barrier(jnp.sum(masked * masked, axis=0))
    scaled = masked * lax.rsqrt(col_total + 1e-06)[None, :]
    pieces = scaled.reshape(PIECES, PIECE, COLS)
    ordered = jnp.take_along_axis(pieces, local_perm[:, :, None].astype(jnp.int32), axis=1)
    arranged = ordered.reshape(2, N_ROW // 2, N_COL, PIECE, COLS)
    onehot = (owner_order[:, :, None] == jnp.arange(N_COL, dtype=jnp.int32)[None, None, :]).astype(jnp.float32)
    placed = jnp.einsum('cjt,chjuk->cthuk', onehot, arranged, precision=lax.Precision.HIGHEST)
    reordered = placed.reshape(2, HALF_ORDER, COLS)
    upper_part = jnp.dot(q_child[:SLAB // 2], reordered[0], precision=lax.Precision.HIGHEST, preferred_element_type=jnp.float32)
    lower_part = jnp.dot(q_child[SLAB // 2:], reordered[1], precision=lax.Precision.HIGHEST, preferred_element_type=jnp.float32)
    return jnp.concatenate([upper_part, lower_part], axis=0)
```

```python
import functools
import jax
import jax.numpy as jnp
from jax import lax
from jax.experimental import pallas as pl
from jax.experimental.pallas import tpu as pltpu
from jax.sharding import PartitionSpec as P

CHUNKS = 8
EDGE_IN, INNER_OWN, INNER_FORWARD, EDGE_OUT, TO_CORE, TO_X, DIAGONAL = range(7)


def passed_along(array, axis, by):
    length = lax.axis_size(axis)
    return lax.ppermute(array, axis, [(i, (i + by) % length) for i in range(length)])


def shifted(array, axis, by):
    length = lax.axis_size(axis)
    pairs = [(i, i + by) for i in range(length) if 0 <= i + by < length]
    return lax.ppermute(array, axis, pairs)


def merge_kernel(chunks, sel_ref, own_ref, q_ref, out_ref, zone, picked, blocks, acc, parts, q_tiles,
                 send_sem, recv_sem, part_send, part_recv, q_sem):
    piece, cols = own_ref.shape
    size = piece // chunks
    out_rows = out_ref.shape[0]
    row = lax.axis_index("row")
    col = lax.axis_index("col")
    place = row % 4
    core_row = row + 1 - 2 * (row % 2)
    x_row = row + 2 - 4 * (place // 2)
    core_place = place + 1 - 2 * (place % 2)
    x_place = place + 2 - 4 * (place // 2)
    diagonal_place = core_place + 2 - 4 * (core_place // 2)
    places = (place, core_place, x_place, diagonal_place)
    on_edge = (col % 3) == 0
    inner = (col % 3) != 0
    opposite = 3 - col
    neighbour = col + 1 - 2 * (col % 2)
    sum_partners = ((col + 2) % 4, opposite, neighbour)

    def rows_of(k):
        return pl.ds(pl.multiple_of(k * size, size), size)

    def copy(kind, k):
        at = rows_of(k)
        source, target, device = {
            EDGE_IN: (own_ref, zone.at[0], {"row": row, "col": neighbour}),
            INNER_OWN: (own_ref, zone.at[1], {"row": row, "col": opposite}),
            INNER_FORWARD: (zone.at[0], zone.at[2], {"row": row, "col": opposite}),
            EDGE_OUT: (picked, zone.at[0], {"row": row, "col": neighbour}),
            TO_CORE: (blocks.at[0], blocks.at[1], {"row": core_row, "col": col}),
            TO_X: (blocks.at[0], blocks.at[2], {"row": x_row, "col": col}),
            DIAGONAL: (blocks.at[2], blocks.at[3], {"row": core_row, "col": col}),
        }[kind]
        return pltpu.make_async_remote_copy(
            src_ref=source.at[at, :], dst_ref=target.at[at, :],
            send_sem=send_sem.at[kind, k], recv_sem=recv_sem.at[kind, k],
            device_id=device, device_id_type=pl.DeviceIdType.MESH)

    def q_copy(k, s):
        slot = (k % 2) * 4 + s
        start = pl.multiple_of(places[s] * piece + k * size, size)
        return pltpu.make_async_copy(q_ref.at[:, pl.ds(start, size)], q_tiles.at[slot], q_sem.at[slot])

    def sum_copy(i):
        start = pl.multiple_of(sum_partners[i] * out_rows, out_rows)
        return pltpu.make_async_remote_copy(
            src_ref=acc.at[pl.ds(start, out_rows), :], dst_ref=parts.at[i],
            send_sem=part_send.at[i], recv_sem=part_recv.at[i],
            device_id={"row": row, "col": sum_partners[i]}, device_id_type=pl.DeviceIdType.MESH)

    for k in range(2):
        for s in range(4):
            q_copy(k, s).start()

    barrier = pltpu.get_barrier_semaphore()
    for partner in sum_partners:
        pl.semaphore_signal(barrier, inc=1, device_id={"row": row, "col": partner},
                            device_id_type=pl.DeviceIdType.MESH)
    for partner in (core_row, x_row):
        pl.semaphore_signal(barrier, inc=1, device_id={"row": partner, "col": col},
                            device_id_type=pl.DeviceIdType.MESH)
    pl.semaphore_wait(barrier, 5)

    def inner_issue(k):
        copy(INNER_OWN, k).start()
        copy(EDGE_IN, k).wait_recv()
        copy(INNER_FORWARD, k).start()

    @pl.when(on_edge)
    def _():
        @pl.loop(0, chunks)
        def _(k):
            copy(EDGE_IN, k).start()

    @pl.when(inner)
    def _():
        inner_issue(0)
        inner_issue(1)

    acc[...] = jnp.zeros_like(acc)

    def split(values):
        high = values.astype(jnp.bfloat16)
        low = (values - high.astype(jnp.float32)).astype(jnp.bfloat16)
        return high, low

    def right_side(k, s):
        high, low = split(blocks[s, rows_of(k), :])
        return jnp.concatenate([high, low, high], axis=0)

    def add_product(k, s, right, start, height):
        at = pl.ds(start, height)
        high, low = split(q_tiles[(k % 2) * 4 + s, at, :])
        left = jnp.concatenate([high, high, low], axis=1)
        acc[at, :] += jnp.dot(left, right, preferred_element_type=jnp.float32)

    @pl.loop(0, chunks + 1)
    def _(k):
        @pl.when(k < chunks)
        def _():
            at = rows_of(k)

            @pl.when(inner)
            def _():
                @pl.when(k + 2 < chunks)
                def _():
                    inner_issue(k + 2)

                copy(INNER_OWN, k).wait_recv()
                copy(INNER_FORWARD, k).wait_recv()
                own, third, fourth = own_ref[at, :], zone[1, at, :], zone[2, at, :]
                for_edge = jnp.broadcast_to(sel_ref[1], own.shape)
                picked[at, :] = jnp.where(for_edge == 2, third, jnp.where(for_edge == 3, fourth, own))
                copy(EDGE_OUT, k).start()
                mine = jnp.broadcast_to(sel_ref[0], own.shape)
                near = jnp.where(mine == 0, own, zone[0, at, :])
                blocks[0, at, :] = jnp.where(mine == 2, third, jnp.where(mine == 3, fourth, near))

            @pl.when(on_edge)
            def _():
                copy(EDGE_OUT, k).wait_recv()
                mine = jnp.broadcast_to(sel_ref[0], (size, cols))
                blocks[0, at, :] = jnp.where(mine == 0, own_ref[at, :], zone[0, at, :])

            copy(TO_X, k).start()
            copy(TO_CORE, k).start()

        @pl.when(k >= 1)
        def _():
            copy(TO_X, k - 1).wait_recv()
            copy(DIAGONAL, k - 1).start()

        @pl.when(k >= 2)
        def _():
            done = k - 2
            copy(TO_CORE, done).wait_recv()
            copy(DIAGONAL, done).wait_recv()
            for s in range(4):
                q_copy(done, s).wait()
                right = right_side(done, s)

                @pl.loop(0, piece // out_rows)
                def _(r):
                    add_product(done, s, right, pl.multiple_of(r * out_rows, out_rows), out_rows)

                @pl.when(done + 2 < chunks)
                def _():
                    q_copy(done + 2, s).start()

    last = chunks - 1
    copy(TO_CORE, last).wait_recv()
    copy(DIAGONAL, last).wait_recv()
    for s in range(4):
        q_copy(last, s).wait()
    for i, target in enumerate(sum_partners + (col,)):
        for s in range(4):
            add_product(last, s, right_side(last, s), pl.multiple_of(target * out_rows, out_rows), out_rows)
        if i < 3:
            sum_copy(i).start()

    total = acc[pl.ds(pl.multiple_of(col * out_rows, out_rows), out_rows), :]
    for i in (2, 1, 0):
        sum_copy(i).wait_recv()
        total = total + parts[i]
    out_ref[...] = total

    for i in range(3):
        sum_copy(i).wait_send()

    @pl.loop(0, chunks)
    def _(k):
        @pl.when(on_edge)
        def _():
            copy(EDGE_IN, k).wait_send()

        @pl.when(inner)
        def _():
            copy(INNER_OWN, k).wait_send()
            copy(INNER_FORWARD, k).wait_send()
            copy(EDGE_OUT, k).wait_send()

        copy(TO_CORE, k).wait_send()
        copy(TO_X, k).wait_send()
        copy(DIAGONAL, k).wait_send()


def merged_by_kernel(q_child, ordered, targets, col_index):
    piece, cols = ordered.shape
    chunks = CHUNKS
    size = piece // chunks
    places = jnp.arange(targets.shape[0], dtype=jnp.int32)
    order = jnp.sum(jnp.where(targets[None, :] == places[:, None], places[None, :], 0), axis=1)
    neighbour = col_index + 1 - 2 * (col_index % 2)
    opposite = 3 - col_index
    inner = (col_index % 3) != 0

    def slot(source):
        far = jnp.where(source == opposite, 2, 3)
        return jnp.where(source == col_index, 0, jnp.where((source == neighbour) | ~inner, 1, far))

    sel = jnp.stack([slot(order[col_index]), slot(order[neighbour])]).astype(jnp.int32)
    out_rows = q_child.shape[0] // 4
    return pl.pallas_call(
        functools.partial(merge_kernel, chunks),
        out_shape=jax.ShapeDtypeStruct((out_rows, cols), jnp.float32),
        in_specs=[pl.BlockSpec(memory_space=pltpu.SMEM), pl.BlockSpec(memory_space=pltpu.VMEM),
                  pl.BlockSpec(memory_space=pl.ANY)],
        out_specs=pl.BlockSpec(memory_space=pltpu.VMEM),
        scratch_shapes=[
            pltpu.VMEM((3, piece, cols), jnp.float32),
            pltpu.VMEM((piece, cols), jnp.float32),
            pltpu.VMEM((4, piece, cols), jnp.float32),
            pltpu.VMEM((q_child.shape[0], cols), jnp.float32),
            pltpu.VMEM((3, out_rows, cols), jnp.float32),
            pltpu.VMEM((8, q_child.shape[0], size), jnp.float32),
            pltpu.SemaphoreType.DMA((7, chunks)),
            pltpu.SemaphoreType.DMA((7, chunks)),
            pltpu.SemaphoreType.DMA((3,)),
            pltpu.SemaphoreType.DMA((3,)),
            pltpu.SemaphoreType.DMA((8,)),
        ],
        compiler_params=pltpu.CompilerParams(
            collective_id=0, has_side_effects=True, vmem_limit_bytes=56 * 1024 * 1024),
        cost_estimate=pl.CostEstimate(
            flops=6 * q_child.shape[0] * q_child.shape[1] * cols,
            bytes_accessed=4 * q_child.shape[0] * q_child.shape[1], transcendentals=0),
    )(sel, ordered, q_child)


def merged_by_rings(q_child, ordered, targets, col_index):
    piece_rows = ordered.shape[0]
    row_count = lax.axis_size("row")
    col_count = lax.axis_size("col")
    half_count = row_count // 2
    place_in_half = lax.axis_index("row") % half_count

    def advance(shifts, carry):
        travel, holding = carry
        travel = passed_along(travel, "col", 1)
        source = (col_index - shifts) % col_count
        holding = jnp.where(targets[source] == col_index, travel, holding)
        return (travel, holding)

    start_hold = jnp.where(targets[col_index] == col_index, ordered, jnp.zeros_like(ordered))
    _, holding = lax.fori_loop(1, col_count, advance, (ordered, start_hold))
    empty_block = jnp.zeros((half_count * piece_rows, holding.shape[1]), holding.dtype)
    own_block = lax.dynamic_update_slice_in_dim(empty_block, holding, place_in_half * piece_rows, 0)

    def collect_step(steps, carry):
        going_up, going_down, block = carry
        going_up = shifted(going_up, "row", 1)
        going_down = shifted(going_down, "row", -1)
        below = place_in_half - steps
        above = place_in_half + steps
        below_slot = jnp.clip(below, 0, half_count - 1)
        above_slot = jnp.clip(above, 0, half_count - 1)
        with_below = lax.dynamic_update_slice_in_dim(block, going_up, below_slot * piece_rows, 0)
        block = jnp.where(below >= 0, with_below, block)
        with_above = lax.dynamic_update_slice_in_dim(block, going_down, above_slot * piece_rows, 0)
        block = jnp.where(above < half_count, with_above, block)
        return (going_up, going_down, block)

    _, _, secular_block = lax.fori_loop(1, half_count, collect_step, (holding, holding, own_block))
    product = jnp.dot(q_child, secular_block, precision=lax.Precision.HIGHEST,
                      preferred_element_type=jnp.float32)
    return lax.psum_scatter(product, "col", scatter_dimension=0, tiled=True)


def per_device(q_child, sec_weights, deflated, local_perm, owner_order):
    kept_rows = (1 - deflated).astype(jnp.float32)[:, None]
    masked = sec_weights * kept_rows
    col_total = lax.psum(jnp.sum(masked * masked, axis=0), ("row", "col"))
    row_count = lax.axis_size("row")
    col_count = lax.axis_size("col")
    child_half = lax.axis_index("row") // (row_count // 2)
    targets = lax.dynamic_index_in_dim(owner_order, child_half, 0, keepdims=False)
    ordered = jnp.take(masked, local_perm[0], axis=0)
    col_index = lax.axis_index("col")
    piece = ordered.shape[0]
    fits = row_count == 8 and col_count == 4 and piece % (CHUNKS * 128) == 0
    merge = merged_by_kernel if fits else merged_by_rings
    merged = merge(q_child, ordered, targets, col_index)
    return merged * lax.rsqrt(col_total + 1e-06)[None, :]


def solution(mesh):
    placed = (
        P("row", "col"),
        P(("row", "col"), None),
        P(("row", "col")),
        P(("row", "col"), None),
        P(),
    )
    return jax.shard_map(
        per_device, mesh=mesh, in_specs=placed, out_specs=P(("row", "col"), None), check_vma=False
    )
```

```python
import functools
import jax
import jax.numpy as jnp
from jax import lax
from jax.experimental import pallas as pl
from jax.experimental.pallas import tpu as pltpu
from jax.sharding import PartitionSpec as P

CHUNKS = 8
EDGE_IN, INNER_OWN, INNER_FORWARD, EDGE_OUT, TO_CORE, TO_X, DIAGONAL = range(7)


def passed_along(array, axis, by):
    length = lax.axis_size(axis)
    return lax.ppermute(array, axis, [(i, (i + by) % length) for i in range(length)])


def shifted(array, axis, by):
    length = lax.axis_size(axis)
    pairs = [(i, i + by) for i in range(length) if 0 <= i + by < length]
    return lax.ppermute(array, axis, pairs)


def merge_kernel(chunks, one_crosses, owner_ref, own_ref, squares_ref, q_ref, out_ref, zone, picked, blocks, acc,
                 parts, q_tiles, sums, sums_in, send_sem, recv_sem, part_send, part_recv, sums_send, sums_recv, q_sem):
    piece, cols = own_ref.shape
    size = piece // chunks
    out_rows = out_ref.shape[0]
    ahead = 1 if one_crosses else 2
    row = lax.axis_index("row")
    col = lax.axis_index("col")
    place = row % 4
    core_row = row + 1 - 2 * (row % 2)
    x_row = row + 2 - 4 * (place // 2)
    core_place = place + 1 - 2 * (place % 2)
    x_place = place + 2 - 4 * (place // 2)
    diagonal_place = core_place + 2 - 4 * (core_place // 2)
    places = (place, core_place, x_place, diagonal_place)
    on_edge = (col % 3) == 0
    inner = (col % 3) != 0
    opposite = 3 - col
    neighbour = col + 1 - 2 * (col % 2)
    skew = (col + 2) % 4
    y_row = row + 4 - 8 * (row // 4)
    child = row // 4
    partners = tuple({"row": r, "col": col} for r in (core_row, x_row, y_row)) + tuple(
        {"row": row, "col": c} for c in (neighbour, opposite))

    def slot_of(target):
        source = 0
        for j in range(4):
            source = source + jnp.where(owner_ref[child, j] == target, j, 0)
        far = jnp.where(source == opposite, 2, 3)
        far = jnp.where(source == neighbour, 1, far)
        return jnp.where(source == col, 0, far)

    my_slot = slot_of(col)
    edge_slot = slot_of(neighbour)
    near_target = owner_ref[child, neighbour]
    low_side = jnp.where(col < 2, 1, 0)
    edge_crosses = jnp.where(near_target < 2, 1 - low_side, low_side)

    def rows_of(k):
        return pl.ds(pl.multiple_of(k * size, size), size)

    def copy(kind, k):
        at = rows_of(k)
        source, target, device = {
            EDGE_IN: (own_ref, zone.at[0], {"row": row, "col": neighbour}),
            INNER_OWN: (zone.at[2] if one_crosses else own_ref, zone.at[1], {"row": row, "col": opposite}),
            INNER_FORWARD: (zone.at[0], zone.at[2], {"row": row, "col": opposite}),
            EDGE_OUT: (picked, zone.at[0], {"row": row, "col": neighbour}),
            TO_CORE: (blocks.at[0], blocks.at[1], {"row": core_row, "col": col}),
            TO_X: (blocks.at[0], blocks.at[2], {"row": x_row, "col": col}),
            DIAGONAL: (blocks.at[2], blocks.at[3], {"row": core_row, "col": col}),
        }[kind]
        return pltpu.make_async_remote_copy(
            src_ref=source.at[at, :], dst_ref=target.at[at, :],
            send_sem=send_sem.at[kind, k], recv_sem=recv_sem.at[kind, k],
            device_id=device, device_id_type=pl.DeviceIdType.MESH)

    def q_copy(k, s):
        slot = (k % 2) * 4 + s
        start = pl.multiple_of(places[s] * piece + k * size, size)
        return pltpu.make_async_copy(q_ref.at[:, pl.ds(start, size)], q_tiles.at[slot], q_sem.at[slot])

    def part_rows(target):
        return pl.ds(pl.multiple_of(target * out_rows, out_rows), out_rows)

    def part_copy(i):
        target, device = ((skew, neighbour), (neighbour, neighbour), (opposite, opposite))[i]
        return pltpu.make_async_remote_copy(
            src_ref=acc.at[part_rows(target), :], dst_ref=parts.at[i],
            send_sem=part_send.at[i], recv_sem=part_recv.at[i],
            device_id={"row": row, "col": device}, device_id_type=pl.DeviceIdType.MESH)

    def sums_copy(i):
        return pltpu.make_async_remote_copy(
            src_ref=sums.at[i], dst_ref=sums_in.at[i], send_sem=sums_send.at[i], recv_sem=sums_recv.at[i],
            device_id=partners[i], device_id_type=pl.DeviceIdType.MESH)

    for k in range(2):
        for s in range(4):
            q_copy(k, s).start()

    barrier = pltpu.get_barrier_semaphore()
    for partner in partners:
        pl.semaphore_signal(barrier, inc=1, device_id=partner, device_id_type=pl.DeviceIdType.MESH)
    sums[0] = jnp.broadcast_to(squares_ref[...], sums.shape[1:])
    pl.semaphore_wait(barrier, 5)

    def inner_issue(k):
        if one_crosses:
            at = rows_of(k)
            copy(EDGE_IN, k).wait_recv()
            crossing = jnp.broadcast_to(edge_crosses, (size, cols))
            zone[2, at, :] = jnp.where(crossing == 1, zone[0, at, :], own_ref[at, :])
            copy(INNER_OWN, k).start()
        else:
            copy(INNER_OWN, k).start()
            copy(EDGE_IN, k).wait_recv()
            copy(INNER_FORWARD, k).start()

    @pl.when(on_edge)
    def _():
        @pl.loop(0, chunks)
        def _(k):
            copy(EDGE_IN, k).start()

    @pl.when(inner)
    def _():
        for k in range(ahead):
            inner_issue(k)

    sums_copy(0).start()
    acc[...] = jnp.zeros_like(acc)

    def split(values):
        high = values.astype(jnp.bfloat16)
        low = (values - high.astype(jnp.float32)).astype(jnp.bfloat16)
        return high, low

    def right_side(k, s):
        high, low = split(blocks[s, rows_of(k), :])
        return jnp.concatenate([high, low, high], axis=0)

    def add_product(k, s, right, start, height):
        at = pl.ds(start, height)
        high, low = split(q_tiles[(k % 2) * 4 + s, at, :])
        left = jnp.concatenate([high, high, low], axis=1)
        acc[at, :] += jnp.dot(left, right, preferred_element_type=jnp.float32)

    @pl.loop(0, chunks + 1)
    def _(k):
        for i in range(4):
            @pl.when(k == i + 1)
            def _():
                sums_copy(i).wait_recv()
                sums[i + 1] = sums[i] + sums_in[i]
                sums_copy(i + 1).start()

        @pl.when(k < chunks)
        def _():
            at = rows_of(k)

            @pl.when(inner)
            def _():
                @pl.when(k + ahead < chunks)
                def _():
                    inner_issue(k + ahead)

                copy(INNER_OWN, k).wait_recv()
                own, third = own_ref[at, :], zone[1, at, :]
                if one_crosses:
                    fourth = third
                else:
                    copy(INNER_FORWARD, k).wait_recv()
                    fourth = zone[2, at, :]
                for_edge = jnp.broadcast_to(edge_slot, own.shape)
                picked[at, :] = jnp.where(for_edge == 2, third, jnp.where(for_edge == 3, fourth, own))
                copy(EDGE_OUT, k).start()
                mine = jnp.broadcast_to(my_slot, own.shape)
                near = jnp.where(mine == 0, own, zone[0, at, :])
                blocks[0, at, :] = jnp.where(mine == 2, third, jnp.where(mine == 3, fourth, near))

            @pl.when(on_edge)
            def _():
                copy(EDGE_OUT, k).wait_recv()
                mine = jnp.broadcast_to(my_slot, (size, cols))
                blocks[0, at, :] = jnp.where(mine == 0, own_ref[at, :], zone[0, at, :])

            copy(TO_X, k).start()
            copy(TO_CORE, k).start()

        @pl.when(k >= 1)
        def _():
            copy(TO_X, k - 1).wait_recv()
            copy(DIAGONAL, k - 1).start()

        @pl.when(k >= 2)
        def _():
            done = k - 2
            copy(TO_CORE, done).wait_recv()
            copy(DIAGONAL, done).wait_recv()
            for s in range(4):
                q_copy(done, s).wait()
                right = right_side(done, s)

                @pl.loop(0, piece // out_rows)
                def _(r):
                    add_product(done, s, right, pl.multiple_of(r * out_rows, out_rows), out_rows)

                @pl.when(done + 2 < chunks)
                def _():
                    q_copy(done + 2, s).start()

    last = chunks - 1
    copy(TO_CORE, last).wait_recv()
    copy(DIAGONAL, last).wait_recv()
    for s in range(4):
        q_copy(last, s).wait()

    def finish(target):
        for s in range(4):
            add_product(last, s, right_side(last, s), pl.multiple_of(target * out_rows, out_rows), out_rows)

    finish(skew)
    part_copy(0).start()
    finish(opposite)
    finish(neighbour)
    part_copy(0).wait_recv()
    acc[part_rows(opposite), :] += parts[0]
    part_copy(2).start()
    part_copy(1).start()
    finish(col)
    sums_copy(4).wait_recv()
    scale = lax.rsqrt(sums[4] + sums_in[4] + 1e-06)[0:1, :]
    part_copy(1).wait_recv()
    part_copy(2).wait_recv()
    out_ref[...] = (acc[part_rows(col), :] + parts[1] + parts[2]) * scale

    for i in range(3):
        part_copy(i).wait_send()
    for i in range(5):
        sums_copy(i).wait_send()

    @pl.loop(0, chunks)
    def _(k):
        @pl.when(on_edge)
        def _():
            copy(EDGE_IN, k).wait_send()

        @pl.when(inner)
        def _():
            copy(INNER_OWN, k).wait_send()
            if not one_crosses:
                copy(INNER_FORWARD, k).wait_send()
            copy(EDGE_OUT, k).wait_send()

        copy(TO_CORE, k).wait_send()
        copy(TO_X, k).wait_send()
        copy(DIAGONAL, k).wait_send()


def merged_by_kernel(one_crosses, owner_order, ordered, squares, q_child):
    piece, cols = ordered.shape
    chunks = CHUNKS
    size = piece // chunks
    out_rows = q_child.shape[0] // 4
    return pl.pallas_call(
        functools.partial(merge_kernel, chunks, one_crosses),
        out_shape=jax.ShapeDtypeStruct((out_rows, cols), jnp.float32),
        in_specs=[pl.BlockSpec(memory_space=pltpu.SMEM), pl.BlockSpec(memory_space=pltpu.VMEM),
                  pl.BlockSpec(memory_space=pltpu.VMEM), pl.BlockSpec(memory_space=pl.ANY)],
        out_specs=pl.BlockSpec(memory_space=pltpu.VMEM),
        scratch_shapes=[
            pltpu.VMEM((3, piece, cols), jnp.float32),
            pltpu.VMEM((piece, cols), jnp.float32),
            pltpu.VMEM((4, piece, cols), jnp.float32),
            pltpu.VMEM((q_child.shape[0], cols), jnp.float32),
            pltpu.VMEM((3, out_rows, cols), jnp.float32),
            pltpu.VMEM((8, q_child.shape[0], size), jnp.float32),
            pltpu.VMEM((5, 8, cols), jnp.float32),
            pltpu.VMEM((5, 8, cols), jnp.float32),
            pltpu.SemaphoreType.DMA((7, chunks)),
            pltpu.SemaphoreType.DMA((7, chunks)),
            pltpu.SemaphoreType.DMA((3,)),
            pltpu.SemaphoreType.DMA((3,)),
            pltpu.SemaphoreType.DMA((5,)),
            pltpu.SemaphoreType.DMA((5,)),
            pltpu.SemaphoreType.DMA((8,)),
        ],
        compiler_params=pltpu.CompilerParams(
            collective_id=1 if one_crosses else 2, has_side_effects=True, vmem_limit_bytes=56 * 1024 * 1024),
        cost_estimate=pl.CostEstimate(
            flops=6 * q_child.shape[0] * q_child.shape[1] * cols,
            bytes_accessed=4 * q_child.shape[0] * q_child.shape[1], transcendentals=0),
    )(owner_order, ordered, squares, q_child)


def merged_by_rings(q_child, ordered, targets, col_index):
    piece_rows = ordered.shape[0]
    row_count = lax.axis_size("row")
    col_count = lax.axis_size("col")
    half_count = row_count // 2
    place_in_half = lax.axis_index("row") % half_count

    def advance(shifts, carry):
        travel, holding = carry
        travel = passed_along(travel, "col", 1)
        source = (col_index - shifts) % col_count
        holding = jnp.where(targets[source] == col_index, travel, holding)
        return (travel, holding)

    start_hold = jnp.where(targets[col_index] == col_index, ordered, jnp.zeros_like(ordered))
    _, holding = lax.fori_loop(1, col_count, advance, (ordered, start_hold))
    empty_block = jnp.zeros((half_count * piece_rows, holding.shape[1]), holding.dtype)
    own_block = lax.dynamic_update_slice_in_dim(empty_block, holding, place_in_half * piece_rows, 0)

    def collect_step(steps, carry):
        going_up, going_down, block = carry
        going_up = shifted(going_up, "row", 1)
        going_down = shifted(going_down, "row", -1)
        below = place_in_half - steps
        above = place_in_half + steps
        below_slot = jnp.clip(below, 0, half_count - 1)
        above_slot = jnp.clip(above, 0, half_count - 1)
        with_below = lax.dynamic_update_slice_in_dim(block, going_up, below_slot * piece_rows, 0)
        block = jnp.where(below >= 0, with_below, block)
        with_above = lax.dynamic_update_slice_in_dim(block, going_down, above_slot * piece_rows, 0)
        block = jnp.where(above < half_count, with_above, block)
        return (going_up, going_down, block)

    _, _, secular_block = lax.fori_loop(1, half_count, collect_step, (holding, holding, own_block))
    product = jnp.dot(q_child, secular_block, precision=lax.Precision.HIGHEST,
                      preferred_element_type=jnp.float32)
    return lax.psum_scatter(product, "col", scatter_dimension=0, tiled=True)


def per_device(q_child, sec_weights, deflated, local_perm, owner_order):
    kept_rows = (1 - deflated).astype(jnp.float32)[:, None]
    masked = sec_weights * kept_rows
    squares = jnp.sum(masked * masked, axis=0)
    row_count = lax.axis_size("row")
    col_count = lax.axis_size("col")
    ordered = masked.at[local_perm[0]].get(mode="promise_in_bounds", unique_indices=True)
    piece = ordered.shape[0]
    if row_count == 8 and col_count == 4 and piece % (CHUNKS * 128) == 0:
        crossing = jnp.sum((owner_order[:, :2] >= 2).astype(jnp.int32), axis=1)
        return lax.cond(
            jnp.max(crossing) <= 1,
            functools.partial(merged_by_kernel, True),
            functools.partial(merged_by_kernel, False),
            owner_order, ordered, squares[None, :], q_child)
    col_total = lax.psum(squares, ("row", "col"))
    child_half = lax.axis_index("row") // (row_count // 2)
    targets = lax.dynamic_index_in_dim(owner_order, child_half, 0, keepdims=False)
    merged = merged_by_rings(q_child, ordered, targets, lax.axis_index("col"))
    return merged * lax.rsqrt(col_total + 1e-06)[None, :]


def solution(mesh):
    placed = (
        P("row", "col"),
        P(("row", "col"), None),
        P(("row", "col")),
        P(("row", "col"), None),
        P(),
    )
    return jax.shard_map(
        per_device, mesh=mesh, in_specs=placed, out_specs=P(("row", "col"), None), check_vma=False
    )
```
